32 devices in a mesh: occ: 2 (over y), aux: 16 (over z, x, core).
Axes of the slice: x: 2, y: 2, z: 4, core: 2. Of those that a mesh axis runs over, the one named last changes fastest.
Arguments:
- factors: float32 [2, 640, 24576], P('occ', None, 'aux'), may hold values from -0.6 to 0.6
- occ_energy: float32 [8], replicated, may hold values from -1.5 to -0.3
- vir_energy: float32 [640], replicated, may hold values from 0.2 to 4
- orbital: int32 [2], replicated, may hold values from 0 to 7
- vir_index: int32 [640], replicated, may hold values from 0 to 639, each once
Outputs:
- density: float32 [2, 640, 24576], P('occ', None, 'aux')
The draws below stay inside these ranges and needn't reach their ends.
Inputs may be any that keep to these rules, and one draw needn't show every extreme that they name: `vir_index`: each virtual's row appears once.
All inputs are finite; a program needn't handle non-finite values.
Results may differ from the reference program's by a relative error of at most 0.0001.
Values sent between devices are 32-bit elements; how exact they have to be, the bound alone decides.
A program may use at most 64 MiB of HBM per device.

```python
import jax
import jax.numpy as jnp
from jax import lax

V = 640
NAUX = 24576
ORBS = 2
OCC_ALL = 8
N_OCC = 2


def strengthened(values, stream_key, source, target, shards_of, factor):
    def block_of(dim):
        return (jnp.arange(values.shape[dim]) // (values.shape[dim] // shards_of)).reshape((-1,) + (1,) * (values.ndim - 1 - dim))

    one_side = jax.random.permutation(stream_key, shards_of)[block_of(target)]
    second = (block_of(target) + shards_of // 2) % shards_of
    return jnp.where((block_of(source) == one_side) | (block_of(source) == second), factor * values, values)


def steps_of(rng, extent, cuts, least, high):
    loudness, own = 1.0, jax.random.fold_in(rng, 6)
    for axis_at, shards_of in cuts:
        draws = jnp.exp(jax.random.uniform(jax.random.fold_in(own, axis_at), (shards_of,), jnp.float32, least / len(cuts), high / len(cuts)))
        loudness = loudness * jnp.repeat(draws, extent[axis_at] // shards_of).reshape([-1 if axis == axis_at else 1 for axis in range(len(extent))])
    return loudness


def noise_with(rng, dims, width, most, shards, heavy, held_as=jnp.bfloat16):
    values = width * jax.random.normal(rng, dims, jnp.float32)
    if shards:
        values = values * steps_of(rng, dims, shards, -0.22, 0.18)
    return jnp.clip(strengthened(values, jax.random.fold_in(rng, 3), *heavy), -most, most).astype(held_as)


def setup_inputs(seed: int = 0) -> dict:
    arg_keys = jax.random.split(jax.random.key(seed), 6)
    factors = noise_with(arg_keys[0], (ORBS, V, NAUX), 0.1, 0.6, ((0, 2), (2, 16)), (2, 1, 16, 2.0), jnp.float32)
    occ_energy = jnp.clip(jax.random.uniform(arg_keys[1], (OCC_ALL,), jnp.float32, -1.5, -0.3), -1.5, -0.3)
    vir_energy = jnp.clip(jax.random.uniform(arg_keys[2], (V,), jnp.float32, 0.2, 4.0), 0.2, 4.0)
    orbital = jax.random.randint(arg_keys[3], (ORBS,), 0, OCC_ALL).astype(jnp.int32)
    vir_index = jax.random.permutation(arg_keys[4], V).astype(jnp.int32)
    return dict(factors=factors, occ_energy=occ_energy, vir_energy=vir_energy, orbital=orbital, vir_index=vir_index)


highest = lax.Precision.HIGHEST


def reference(factors, occ_energy, vir_energy, orbital, vir_index):
    virtual_energy = vir_energy[vir_index]
    orbital_energy = occ_energy[orbital]
    totals = [jnp.zeros((V, NAUX), jnp.float32) for _ in range(N_OCC)]
    for first in range(N_OCC):
        for offset in (1, 3):
            second = (first + offset) % N_OCC
            integrals = lax.dot_general(factors[first], factors[second], (((1,), (1,)), ((), ())), precision=highest, preferred_element_type=jnp.float32)
            denominator = orbital_energy[first] + orbital_energy[second] - virtual_energy[:, None] - virtual_energy[None, :]
            amplitude = integrals / denominator
            totals[first] = totals[first] + jnp.dot(amplitude, factors[second], precision=highest, preferred_element_type=jnp.float32)
            totals[second] = totals[second] + lax.dot_general(amplitude, factors[first], (((0,), (0,)), ((), ())), precision=highest, preferred_element_type=jnp.float32)
    return jnp.stack(totals)
```

```python
import jax
import jax.numpy as jnp
from jax import lax
from jax.sharding import PartitionSpec as P

exact = lax.Precision.HIGH
OFFSETS = (1, 3)


def passed_along(value, axis, steps):
    count = lax.axis_size(axis)
    pairs = [(source, (source + steps) % count) for source in range(count)]
    return lax.ppermute(value, axis, pairs)


def contract(left, right, dims):
    return lax.dot_general(left, right, (dims, ((), ())), precision=exact, preferred_element_type=jnp.float32)


def table_pick(table, indices):
    matches = indices[:, None] == jnp.arange(table.shape[0], dtype=jnp.int32)[None, :]
    return jnp.sum(jnp.where(matches, table[None, :], 0.0), axis=1)


def scalar_pick(values, position):
    matches = jnp.arange(values.shape[0], dtype=jnp.int32) == position
    return jnp.sum(jnp.where(matches, values, 0.0))


def energies(occ_energy, vir_energy, orbital, vir_index):
    return table_pick(vir_energy, vir_index), table_pick(occ_energy, orbital)


def denominator_for(energy_first, energy_second, virtual_energy):
    return energy_first + energy_second - virtual_energy[:, None] - virtual_energy[None, :]


def general_body(factors, occ_energy, vir_energy, orbital, vir_index):
    local_factor = factors[0]
    group_index = lax.axis_index("occ")
    group_count = lax.axis_size("occ")
    virtual_energy, orbital_energy = energies(occ_energy, vir_energy, orbital, vir_index)
    energy_self = scalar_pick(orbital_energy, group_index)
    totals = jnp.zeros_like(local_factor)
    for offset in OFFSETS:
        energy_other = scalar_pick(orbital_energy, (group_index + offset) % group_count)
        partner = passed_along(local_factor, "occ", -offset)
        summed = lax.psum(contract(local_factor, partner, ((1,), (1,))), "aux")
        amplitude = summed / denominator_for(energy_self, energy_other, virtual_energy)
        back = passed_along(contract(amplitude, local_factor, ((0,), (0,))), "occ", offset)
        totals = totals + contract(amplitude, partner, ((1,), (0,))) + back
    return totals[None]


def paired_body(factors, occ_energy, vir_energy, orbital, vir_index):
    local_factor = factors[0]
    half = local_factor.shape[1] // 2
    group = lax.axis_index("occ")
    virtual_energy, orbital_energy = energies(occ_energy, vir_energy, orbital, vir_index)
    denominator = denominator_for(orbital_energy[0], orbital_energy[1], virtual_energy)
    mine = lax.dynamic_slice_in_dim(local_factor, group * half, half, 1)
    other = lax.dynamic_slice_in_dim(local_factor, (1 - group) * half, half, 1)
    first = passed_along(other, "occ", 1)
    partial = contract(mine, first, ((1,), (1,)))
    partial = jnp.where(group == 0, partial, partial.T)
    second = passed_along(mine, "occ", 1)
    summed = lax.psum(partial, ("occ", "aux"))
    amplitude = (2.0 * len(OFFSETS)) * summed / denominator
    amplitude = jnp.where(group == 0, amplitude, amplitude.T)
    here = contract(amplitude, first, ((1,), (0,)))
    there = contract(amplitude, second, ((1,), (0,)))
    low = jnp.where(group == 0, here, there)
    high = jnp.where(group == 0, there, here)
    return jnp.concatenate([low, high], axis=1)[None]


def solution(mesh):
    paired = mesh.shape["occ"] == 2 and all(offset % 2 for offset in OFFSETS)
    return jax.shard_map(
        paired_body if paired else general_body,
        mesh=mesh,
        in_specs=(P("occ", None, "aux"), P(), P(), P(), P()),
        out_specs=P("occ", None, "aux"),
        check_vma=False,
    )
```

```python
import functools

import jax
import jax.numpy as jnp
from jax import lax
from jax.experimental import pallas as pl
from jax.experimental.pallas import tpu as pltpu
from jax.sharding import PartitionSpec as P

exact = lax.Precision.HIGH
OFFSETS = (1, 3)
MESH = pl.DeviceIdType.MESH
SUB = 8
BLOCK = 128
AHEAD = 2


def passed_along(value, axis, steps):
    count = lax.axis_size(axis)
    pairs = [(source, (source + steps) % count) for source in range(count)]
    return lax.ppermute(value, axis, pairs)


def contract(left, right, dims):
    return lax.dot_general(left, right, (dims, ((), ())), precision=exact, preferred_element_type=jnp.float32)


def table_pick(table, indices):
    matches = indices[:, None] == jnp.arange(table.shape[0], dtype=jnp.int32)[None, :]
    return jnp.sum(jnp.where(matches, table[None, :], 0.0), axis=1)


def scalar_pick(values, position):
    matches = jnp.arange(values.shape[0], dtype=jnp.int32) == position
    return jnp.sum(jnp.where(matches, values, 0.0))


def energies(occ_energy, vir_energy, orbital, vir_index):
    return table_pick(vir_energy, vir_index), table_pick(occ_energy, orbital)


def denominator_for(energy_first, energy_second, virtual_energy):
    return energy_first + energy_second - virtual_energy[:, None] - virtual_energy[None, :]


def general_body(factors, occ_energy, vir_energy, orbital, vir_index):
    local_factor = factors[0]
    group_index = lax.axis_index("occ")
    group_count = lax.axis_size("occ")
    virtual_energy, orbital_energy = energies(occ_energy, vir_energy, orbital, vir_index)
    energy_self = scalar_pick(orbital_energy, group_index)
    totals = jnp.zeros_like(local_factor)
    for offset in OFFSETS:
        energy_other = scalar_pick(orbital_energy, (group_index + offset) % group_count)
        partner = passed_along(local_factor, "occ", -offset)
        summed = lax.psum(contract(local_factor, partner, ((1,), (1,))), "aux")
        amplitude = summed / denominator_for(energy_self, energy_other, virtual_energy)
        back = passed_along(contract(amplitude, local_factor, ((0,), (0,))), "occ", offset)
        totals = totals + contract(amplitude, partner, ((1,), (0,))) + back
    return totals[None]


def paired_body(factors, occ_energy, vir_energy, orbital, vir_index):
    local_factor = factors[0]
    half = local_factor.shape[1] // 2
    group = lax.axis_index("occ")
    virtual_energy, orbital_energy = energies(occ_energy, vir_energy, orbital, vir_index)
    denominator = denominator_for(orbital_energy[0], orbital_energy[1], virtual_energy)
    mine = lax.dynamic_slice_in_dim(local_factor, group * half, half, 1)
    other = lax.dynamic_slice_in_dim(local_factor, (1 - group) * half, half, 1)
    first = passed_along(other, "occ", 1)
    partial = contract(mine, first, ((1,), (1,)))
    partial = jnp.where(group == 0, partial, partial.T)
    second = passed_along(mine, "occ", 1)
    summed = lax.psum(partial, ("occ", "aux"))
    amplitude = (2.0 * len(OFFSETS)) * summed / denominator
    amplitude = jnp.where(group == 0, amplitude, amplitude.T)
    here = contract(amplitude, first, ((1,), (0,)))
    there = contract(amplitude, second, ((1,), (0,)))
    low = jnp.where(group == 0, here, there)
    high = jnp.where(group == 0, there, here)
    return jnp.concatenate([low, high], axis=1)[None]


def halves(value):
    high = value.astype(jnp.bfloat16)
    return high, (value - high.astype(jnp.float32)).astype(jnp.bfloat16)


def three_pass(left, right, dims):
    dot = functools.partial(lax.dot_general, dimension_numbers=(dims, ((), ())), preferred_element_type=jnp.float32)
    return dot(left[0], right[1]) + dot(left[1], right[0]) + dot(left[0], right[0])


def paired_kernel(
    occ_energy, orbital, vir_energy, vir_index, factors, out,
    own, own_high, own_low, near, near_high, near_low, late,
    parts, landed, sums, sums_other, gathered, amp_high, amp_low, virtual_cols, dense_near, dense_late,
    local_sem, out_sem, y_send, y_recv, part_send, part_recv, sum_send, sum_recv,
    gather_send, gather_recv, forward_send,
):
    group, me = lax.axis_index("occ"), lax.axis_index("aux")
    peers = lax.axis_size("aux")
    partner = 1 - group
    sibling = me + 1 - 2 * lax.rem(me, 2)
    rows, half = own.shape
    blocks = rows // BLOCK
    near_cols = pl.ds(pl.multiple_of(group * half, BLOCK), half)
    late_cols = pl.ds(pl.multiple_of(partner * half, BLOCK), half)

    def chunk(at):
        return pl.ds(at * BLOCK, BLOCK)

    load = pltpu.make_async_copy(factors.at[0, :, near_cols], own, local_sem)
    load.start()

    barrier = pltpu.get_barrier_semaphore()
    pl.semaphore_signal(barrier, inc=1, device_id=(partner, me), device_id_type=MESH)

    def greet(step, carry):
        pl.semaphore_signal(barrier, inc=1, device_id=(group, lax.rem(me + step, peers)), device_id_type=MESH)
        return carry

    lax.fori_loop(1, peers, greet, 0)
    pl.semaphore_wait(barrier, peers)

    def y_copy(at):
        early = at < blocks
        piece = chunk(at % blocks)
        return pltpu.make_async_remote_copy(
            src_ref=factors.at[0, piece, late_cols if early else near_cols],
            dst_ref=(near if early else late).at[piece],
            send_sem=y_send.at[at], recv_sem=y_recv.at[at],
            device_id=(partner, me), device_id_type=MESH,
        )

    def part_copy(at, target, slot):
        return pltpu.make_async_remote_copy(
            src_ref=parts.at[at, target], dst_ref=landed.at[at, slot],
            send_sem=part_send.at[at, target], recv_sem=part_recv.at[at, slot],
            device_id=(group, target), device_id_type=MESH,
        )

    def sum_copy(at):
        return pltpu.make_async_remote_copy(
            src_ref=sums.at[at], dst_ref=sums_other.at[at],
            send_sem=sum_send.at[at], recv_sem=sum_recv.at[at],
            device_id=(partner, me), device_id_type=MESH,
        )

    def gather_copy(slot, target, sem):
        return pltpu.make_async_remote_copy(
            src_ref=gathered.at[slot], dst_ref=gathered.at[slot],
            send_sem=sem, recv_sem=gather_recv.at[slot],
            device_id=(group, target), device_id_type=MESH,
        )

    def add_up(at):
        landed[at, me] = parts[at, me]

        def arrived(step, carry):
            source = lax.rem(me + step, peers)
            part_copy(at, source, source).wait_recv()
            return carry

        lax.fori_loop(1, peers, arrived, 0)
        sums[at] = jnp.sum(landed[at], axis=0)
        sum_copy(at).start()

    for at in range(AHEAD):
        y_copy(at).start()

    table = jnp.broadcast_to(vir_energy[...], (BLOCK, rows)).T
    matches = lax.broadcasted_iota(jnp.int32, (rows, rows), 0) == vir_index[...]
    virtual_row = jnp.sum(jnp.where(matches, table[:, :1], 0.0), axis=0, keepdims=True)
    virtual_cols[...] = jnp.broadcast_to(virtual_row, (BLOCK, rows)).T
    pair_energy = occ_energy[orbital[0]] + occ_energy[orbital[1]]

    load.wait()
    own_high[...], own_low[...] = halves(own[...])

    for at in range(blocks):
        piece = chunk(at)
        y_copy(at).wait_recv()
        y_copy(at + AHEAD).start()
        high, low = halves(near[piece])
        near_high[piece], near_low[piece] = high, low

        @pl.when(group == 0)
        def _():
            product = three_pass((own_high[...], own_low[...]), (high, low), ((1,), (1,)))
            for block in range(blocks):
                for slot in range(BLOCK // SUB):
                    start = block * BLOCK + slot * SUB
                    parts[at, slot, block] = product[start:start + SUB]

        @pl.when(group != 0)
        def _():
            product = three_pass((high, low), (own_high[...], own_low[...]), ((1,), (1,)))
            for block in range(blocks):
                for slot in range(BLOCK // SUB):
                    parts[at, slot, block] = product[slot * SUB:(slot + 1) * SUB, block * BLOCK:(block + 1) * BLOCK]

        def spread(step, carry):
            part_copy(at, lax.rem(me + step, peers), me).start()
            return carry

        lax.fori_loop(1, peers, spread, 0)
        if at:
            add_up(at - 1)
    add_up(blocks - 1)

    for at in range(blocks):
        sum_copy(at).wait_recv()
    for at in range(blocks + AHEAD, 2 * blocks):
        y_copy(at).start()
    for first in range(blocks):
        for second in range(blocks):
            gathered[me, first, second] = sums[first, second] + sums_other[second, first]

    def publish(step, carry):
        gather_copy(me, lax.rem(me + 2 * step, peers), gather_send.at[step]).start()
        return carry

    lax.fori_loop(1, peers // 2, publish, 0)
    gather_copy(me, sibling, gather_send.at[0]).start()

    def pass_on(step, carry):
        source = lax.rem(me + 2 * step, peers)
        gather_copy(source, sibling, forward_send.at[step]).wait_recv()
        gather_copy(source, sibling, forward_send.at[step]).start()
        return carry

    lax.fori_loop(1, peers // 2, pass_on, 0)

    def passed(step, carry):
        source = lax.rem(sibling + 2 * step, peers)
        gather_copy(source, sibling, forward_send.at[0]).wait_recv()
        return carry

    lax.fori_loop(0, peers // 2, passed, 0)

    for first in range(blocks):
        for second in range(blocks):
            block = gathered[:, first, second].reshape(BLOCK, BLOCK)
            block = jnp.where(group == 0, block, block.T)
            below = pair_energy - virtual_cols[chunk(second)] - virtual_cols[chunk(first)].T
            high, low = halves((2.0 * len(OFFSETS)) * block / below)
            amp_high[chunk(second), chunk(first)] = high
            amp_low[chunk(second), chunk(first)] = low

    dense_near[...] = three_pass(
        (amp_high[...], amp_low[...]), (near_high[...], near_low[...]), ((1,), (0,))
    )
    store_near = pltpu.make_async_copy(dense_near, out.at[0, :, near_cols], local_sem)
    store_near.start()
    for at in range(blocks):
        piece = chunk(at)
        y_copy(blocks + at).wait_recv()
        term = three_pass((amp_high[:, piece], amp_low[:, piece]), halves(late[piece]), ((1,), (0,)))
        if at:
            dense_late[...] += term
        else:
            dense_late[...] = term
    store_late = pltpu.make_async_copy(dense_late, out.at[0, :, late_cols], out_sem)
    store_late.start()

    for at in range(2 * blocks):
        y_copy(at).wait_send()
    for at in range(blocks):
        sum_copy(at).wait_send()

        def left(step, carry):
            part_copy(at, lax.rem(me + step, peers), me).wait_send()
            return carry

        lax.fori_loop(1, peers, left, 0)

    def published(step, carry):
        gather_copy(me, sibling, gather_send.at[step]).wait_send()
        return carry

    lax.fori_loop(0, peers // 2, published, 0)

    def forwarded(step, carry):
        gather_copy(me, sibling, forward_send.at[step]).wait_send()
        return carry

    lax.fori_loop(1, peers // 2, forwarded, 0)
    store_near.wait()
    store_late.wait()


def kernel_body(factors, occ_energy, vir_energy, orbital, vir_index):
    _, rows, cols = factors.shape
    half, blocks, peers = cols // 2, rows // BLOCK, lax.axis_size("aux")
    f32, bf16 = jnp.float32, jnp.bfloat16
    vmem, dma = pltpu.VMEM, pltpu.SemaphoreType.DMA
    small = pl.BlockSpec(memory_space=pltpu.VMEM)
    scalars = pl.BlockSpec(memory_space=pltpu.SMEM)
    large = pl.BlockSpec(memory_space=pl.ANY)
    tiles = (blocks, SUB, BLOCK)
    return pl.pallas_call(
        paired_kernel,
        out_shape=jax.ShapeDtypeStruct(factors.shape, f32),
        in_specs=[scalars, scalars, small, small, large],
        out_specs=large,
        scratch_shapes=[
            vmem((rows, half), f32), vmem((rows, half), bf16), vmem((rows, half), bf16),
            vmem((rows, half), f32), vmem((rows, half), bf16), vmem((rows, half), bf16),
            vmem((rows, half), f32),
            vmem((blocks, peers) + tiles, f32), vmem((blocks, peers) + tiles, f32),
            vmem((blocks,) + tiles, f32), vmem((blocks,) + tiles, f32),
            vmem((peers, blocks) + tiles, f32),
            vmem((rows, rows), bf16), vmem((rows, rows), bf16), vmem((rows, BLOCK), f32),
            vmem((rows, half), f32), vmem((rows, half), f32),
            dma, dma, dma((2 * blocks,)), dma((2 * blocks,)),
            dma((blocks, peers)), dma((blocks, peers)), dma((blocks,)), dma((blocks,)),
            dma((peers // 2,)), dma((peers,)), dma((peers // 2,)),
        ],
        compiler_params=pltpu.CompilerParams(
            collective_id=0, has_side_effects=True, vmem_limit_bytes=50 * 2**20
        ),
        cost_estimate=pl.CostEstimate(
            flops=3 * rows * rows * cols * 3, bytes_accessed=3 * rows * cols * 4, transcendentals=0
        ),
    )(occ_energy, orbital, vir_energy[None], vir_index[None], factors)


def fits_kernel(mesh, shape):
    peers, (_, rows, cols) = mesh.shape["aux"], shape
    return peers * SUB == BLOCK and rows % BLOCK == 0 and cols % (2 * BLOCK * peers) == 0


def solution(mesh):
    paired = mesh.shape["occ"] == 2 and all(offset % 2 for offset in OFFSETS)

    def whole(factors, *tables):
        body = general_body
        if paired:
            body = kernel_body if fits_kernel(mesh, factors.shape) else paired_body
        return jax.shard_map(
            body,
            mesh=mesh,
            in_specs=(P("occ", None, "aux"), P(), P(), P(), P()),
            out_specs=P("occ", None, "aux"),
            check_vma=False,
        )(factors, *tables)

    return whole
```
